32 devices in a mesh: dp: 4 (over y, x), ctx: 2 (over core), mp: 4 (over z).
Axes of the slice: x: 2, y: 2, z: 4, core: 2. Of those that a mesh axis runs over, the one named last changes fastest.
Arguments:
- queries: bfloat16 [8192, 2048], P(('dp', 'ctx'), 'mp'), parts along dimension 0, may hold values from -6 to 6
- keys: bfloat16 [8192, 2048], P(('dp', 'ctx'), 'mp'), parts along dimension 0, may hold values from -6 to 6
- values: bfloat16 [8192, 2048], P(('dp', 'ctx'), 'mp'), parts along dimension 0, may hold values from -6 to 6
- segment_ids: int32 [8192], P(('dp', 'ctx')), parts along dimension 0, may hold values from 0 to 5, never falling along the last dimension, each value on 1 to 1024 neighbouring positions
- norm_gain: float32 [2048], P('mp'), may hold values from 0.5 to 1.5
- out_weight: bfloat16 [2048, 4096], P(None, 'mp'), may hold values from -0.125 to 0.125
Outputs:
- projected: bfloat16 [8192, 4096], P(('dp', 'ctx'), 'mp'), parts along dimension 0
The draws below stay inside these ranges and needn't reach their ends.
There are 4 independent parts, one for each index of `dp`. The reference program is written for one: setup_inputs(seed, part) draws one part's arguments, and reference() takes and returns one part's arrays. A program takes and returns all parts, laid end to end along the dimension named above; an argument that names none is the same for every part. Nothing has to cross between parts.
Inputs may be any that keep to these rules, and one draw needn't show every extreme that they name: `segment_ids`: ids never fall along the stream; 6 segments, each of 1 to 1024 consecutive positions, one of exactly 1024.
All inputs are finite; a program needn't handle non-finite values.
Results may differ from the reference program's by a relative error of at most 0.0053.
Values may be sent and summed in bfloat16 or wider, within the bound.
A program may use at most 64 MiB of HBM per device.

```python
import math
import jax
import jax.numpy as jnp
import numpy as np
from jax import lax

D = 4096
HEAD = 128
H = 16
TOK_DEV = 1024
SEGS = 6
HD = 2048
LENGTH = 2048
SEG_MOST = 1024
N_CTX = 2


def block_scale(rng, extent, shards, least, high):
    level, own = 1.0, jax.random.fold_in(rng, 6)
    for dim, shards_of in shards:
        steps = jnp.exp(jax.random.uniform(jax.random.fold_in(own, dim), (shards_of,), jnp.float32, least / len(shards), high / len(shards)))
        level = level * jnp.repeat(steps, extent[dim] // shards_of).reshape([-1 if axis == dim else 1 for axis in range(len(extent))])
    return level


def length_profile(amount, total, reach, slope):
    loads = [(1 << 20) // math.isqrt(standing ** slope) + 1 for standing in range(2, amount + 1)]
    surplus, given = total - reach - (amount - 1), [1] * (amount - 1)
    while surplus > 0:
        candidates = [i for i in range(amount - 1) if given[i] < reach]
        pool, remaining = sum([loads[i] for i in candidates]), surplus
        for i in candidates:
            extra = min(reach - given[i], max(1, remaining * loads[i] // pool), surplus)
            given[i] = given[i] + extra
            surplus = surplus - extra
    return np.array([reach] + given)


def uneven(rng, amount, total, bound, slope):
    if amount == 2:
        one = jax.random.randint(rng, (), max(1, total - bound), min(bound, total - 1) + 1)
        return jnp.stack([one, total - one])
    tallies = jnp.asarray(length_profile(amount, total, bound, slope), jnp.int32)
    couples = (amount - 1) // 2
    source_of, taker = tallies[1:1 + 2 * couples:2], tallies[2:2 + 2 * couples:2]
    room = jnp.minimum(source_of - 1, bound - taker)
    passed = jax.random.randint(jax.random.fold_in(rng, 1), (couples,), 0, 1 << 20) % (room + 1)
    tallies = tallies.at[1:1 + 2 * couples:2].set(source_of - passed).at[2:2 + 2 * couples:2].set(taker + passed)
    return tallies[jax.random.permutation(jax.random.fold_in(rng, 2), amount)]


def centred(key, extent, width, most, split=(), kind=jnp.bfloat16):
    result = jax.random.normal(key, extent, jnp.float32) * width
    if len(split) > 0:
        result = block_scale(key, extent, split, -0.22, 0.18) * result
    return jnp.clip(result, min=-most, max=most).astype(kind)


def setup_inputs(seed: int = 0, part: int = 0) -> dict:
    seeds = jax.random.split(jax.random.key(seed), 7)
    own_keys = jax.random.split(jax.random.fold_in(seeds[6], part), 7)
    return {
        "queries": centred(own_keys[0], (LENGTH, HD), 1.0, 6.0, ((0, 2), (1, 4))),
        "keys": centred(own_keys[1], (LENGTH, HD), 1.0, 6.0, ((0, 2), (1, 4))),
        "values": centred(own_keys[2], (LENGTH, HD), 1.0, 6.0, ((0, 2), (1, 4))),
        "segment_ids": jnp.searchsorted(jnp.cumsum(uneven(own_keys[3], SEGS, LENGTH, SEG_MOST, 1)), jnp.arange(LENGTH), side="right").astype(jnp.int32),
        "norm_gain": jnp.clip(1.0 + 0.1 * jax.random.normal(seeds[4], (HD,), jnp.float32), 0.5, 1.5),
        "out_weight": centred(seeds[5], (HD, D), HD ** -0.5, 0.125, ((1, 4),)),
    }


def features(raw_input):
    return (jax.nn.elu(raw_input.astype(jnp.float32)) + 1.0).astype(jnp.bfloat16)

def reference(queries, keys, values, segment_ids, norm_gain, out_weight):
    feat_query = features(queries).reshape(N_CTX, TOK_DEV, H, HEAD)
    feat_key = features(keys).reshape(N_CTX, TOK_DEV, H, HEAD)
    value_heads = values.reshape(N_CTX, TOK_DEV, H, HEAD)
    segment = segment_ids.reshape(N_CTX, TOK_DEV)
    position = jnp.arange(TOK_DEV)
    causal = position[None, :] <= position[:, None]
    gain_heads = norm_gain.astype(jnp.float32).reshape(H, HEAD)

    def one_block(carry, pieces):
        state_sum, final_seg = carry
        block_query, block_key, block_value, block_seg = pieces
        carry_on = (block_seg == final_seg).astype(jnp.float32)
        allowed = causal & (block_seg[:, None] == block_seg[None, :])
        scores = jnp.einsum('thd,shd->hts', block_query.astype(jnp.float32), block_key.astype(jnp.float32))
        weights = jnp.where(allowed[None], scores, 0.0).astype(jnp.bfloat16)
        inside = jnp.einsum('hts,she->the', weights.astype(jnp.float32), block_value.astype(jnp.float32))
        state_hi = state_sum.astype(jnp.bfloat16)
        state_lo = (state_sum - state_hi.astype(jnp.float32)).astype(jnp.bfloat16)
        query_wide = block_query.astype(jnp.float32)
        carried = jnp.einsum('thd,hde->the', query_wide, state_hi.astype(jnp.float32)) + jnp.einsum('thd,hde->the', query_wide, state_lo.astype(jnp.float32))
        numerator = inside + carry_on[:, None, None] * carried
        normed = numerator * lax.rsqrt(lax.optimization_barrier(jnp.mean(numerator * numerator, axis=-1, keepdims=True)) + 1e-06)
        hidden = (normed * gain_heads[None]).astype(jnp.bfloat16).reshape(TOK_DEV, HD)
        block_last = block_seg[-1]
        in_final = (block_seg == block_last).astype(jnp.float32)
        local_sum = jnp.einsum('thd,the->hde', block_key.astype(jnp.float32) * in_final[:, None, None], block_value.astype(jnp.float32))
        state_sum = local_sum + jnp.where(block_last == final_seg, state_sum, 0.0)
        return ((state_sum, block_last), hidden)
    initial = (jnp.zeros((H, HEAD, HEAD), jnp.float32), jnp.int32(-1))
    _, hidden_all = lax.scan(one_block, initial, (feat_query, feat_key, value_heads, segment))
    hidden_all = hidden_all.reshape(LENGTH, HD)
    return jnp.dot(hidden_all, out_weight, preferred_element_type=jnp.float32).astype(jnp.bfloat16)
```

```python
import functools

import jax
import jax.numpy as jnp
from jax import lax
from jax.experimental import pallas as pl
from jax.experimental.pallas import tpu as pltpu
from jax.sharding import PartitionSpec as P

HEAD = 128
MESH = pl.DeviceIdType.MESH
F32, BF16 = jnp.float32, jnp.bfloat16


def features(raw):
    x = raw.astype(F32)
    return jnp.where(x > 0, x + 1.0, jnp.exp(jnp.minimum(x, 0.0))).astype(BF16)


def nn(a, b):
    return lax.dot_general(a, b, (((1,), (0,)), ((), ())), preferred_element_type=F32)


def nt(a, b):
    return lax.dot_general(a, b, (((1,), (1,)), ((), ())), preferred_element_type=F32)


def tn(a, b):
    return lax.dot_general(a, b, (((0,), (0,)), ((), ())), preferred_element_type=F32)


def kernel(n_ctx, n_mp, chunk, q_hbm, k_hbm, v_hbm, seg_ref, gain_ref, w_hbm, out_hbm,
           q, k, v, w, seg_col, mask, state, carry, hid, out_buf,
           load_sem, out_sem, st_send, st_recv, h_send, h_recv):
    ctx, mp = lax.axis_index("ctx"), lax.axis_index("mp")
    rows, width = q.shape
    heads = width // HEAD
    n_chunk = rows // chunk
    loads = []
    for i, (src, dst) in enumerate(((k_hbm, k), (v_hbm, v), (q_hbm, q), (w_hbm, w))):
        c = pltpu.make_async_copy(src, dst, load_sem.at[i])
        c.start()
        loads.append(c)
    barrier = pltpu.get_barrier_semaphore()
    for d in range(1, n_mp):
        pl.semaphore_signal(barrier, inc=1, device_id={"mp": lax.rem(mp + d, n_mp)}, device_id_type=MESH)
    for d in range(1, n_ctx):
        pl.semaphore_signal(barrier, inc=1, device_id={"ctx": lax.rem(ctx + d, n_ctx)}, device_id_type=MESH)

    seg_row = seg_ref[...].astype(F32)
    seg_col[...] = jnp.transpose(jnp.broadcast_to(seg_row, (HEAD, rows)))
    first = seg_col[0:1, :]
    last = seg_col[rows - 1:rows, :]
    in_final = (seg_col[...] == last).astype(BF16)

    loads[0].wait()
    k[...] = features(k[...])
    loads[1].wait()
    for h in range(heads):
        cols = slice(h * HEAD, (h + 1) * HEAD)
        state[ctx, h * HEAD:(h + 1) * HEAD, :] = tn(k[:, cols] * in_final, v[:, cols])
    state[ctx, width:width + 8, :] = jnp.broadcast_to(last, (8, HEAD))
    pl.semaphore_wait(barrier, n_mp - 1 + n_ctx - 1)
    st_copies = []
    for d in range(1, n_ctx):
        c = pltpu.make_async_remote_copy(
            src_ref=state.at[ctx], dst_ref=state.at[ctx], send_sem=st_send.at[d - 1], recv_sem=st_recv.at[d - 1],
            device_id={"ctx": lax.rem(ctx + d, n_ctx)}, device_id_type=MESH)
        c.start()
        st_copies.append(c)

    for i in range(n_chunk):
        r0, r1 = i * chunk, (i + 1) * chunk
        for j in range(r1 // HEAD):
            s0 = j * HEAD
            t = lax.broadcasted_iota(jnp.int32, (chunk, HEAD), 0) + r0
            s = lax.broadcasted_iota(jnp.int32, (chunk, HEAD), 1) + s0
            same = seg_col[r0:r1, :] == seg_row[:, s0:s0 + HEAD]
            mask[r0:r1, s0:s0 + HEAD] = jnp.where(same & (s <= t), 1.0, 0.0).astype(BF16)
    loads[2].wait()
    q[...] = features(q[...])

    for c in st_copies:
        c.wait()
    total = jnp.zeros((width, HEAD), F32)
    for j in range(n_ctx):
        link = (state[j, width:width + 1, :] == first).astype(F32) * (j < ctx).astype(F32)
        total = total + state[j, 0:width, :] * link
    hi = total.astype(BF16)
    carry[:, 0:HEAD] = hi
    carry[:, HEAD:2 * HEAD] = (total - hi.astype(F32)).astype(BF16)

    h_copies = []
    for i in range(n_chunk):
        r0, r1 = i * chunk, (i + 1) * chunk
        on = (seg_col[r0:r1, :] == first).astype(F32)
        for h in range(heads):
            cols = slice(h * HEAD, (h + 1) * HEAD)
            fq = q[r0:r1, cols]
            score = nt(fq, k[0:r1, cols]).astype(BF16) * mask[r0:r1, 0:r1]
            inside = nn(score, v[0:r1, cols])
            both = nn(fq, carry[cols, :])
            numer = inside + on * (both[:, 0:HEAD] + both[:, HEAD:2 * HEAD])
            mean = jnp.mean(numer * numer, axis=-1, keepdims=True)
            hid[mp, r0:r1, cols] = (numer * lax.rsqrt(mean + 1e-6) * gain_ref[:, cols]).astype(BF16)
        for d in range(1, n_mp):
            c = pltpu.make_async_remote_copy(
                src_ref=hid.at[mp, pl.ds(r0, chunk)], dst_ref=hid.at[mp, pl.ds(r0, chunk)],
                send_sem=h_send.at[d - 1, i], recv_sem=h_recv.at[d - 1, i],
                device_id={"mp": lax.rem(mp + d, n_mp)}, device_id_type=MESH)
            c.start()
            h_copies.append(c)

    loads[3].wait()
    outs = []
    for i in range(n_chunk):
        r0, r1 = i * chunk, (i + 1) * chunk
        for d in range(1, n_mp):
            h_copies[i * (n_mp - 1) + d - 1].wait_recv()
        acc = nn(hid[0, r0:r1, :], w[0:width, :])
        for p in range(1, n_mp):
            acc = acc + nn(hid[p, r0:r1, :], w[p * width:(p + 1) * width, :])
        out_buf[r0:r1, :] = acc.astype(BF16)
        c = pltpu.make_async_copy(out_buf.at[pl.ds(r0, chunk)], out_hbm.at[pl.ds(r0, chunk)], out_sem.at[i])
        c.start()
        outs.append(c)
    for c in h_copies:
        c.wait_send()
    for c in outs:
        c.wait()


def per_device(queries, keys, values, segment_ids, norm_gain, out_weight):
    n_ctx, n_mp = lax.axis_size("ctx"), lax.axis_size("mp")
    rows, width = queries.shape
    cols = out_weight.shape[1]
    chunk = 256
    n_chunk = rows // chunk
    any_spec = pl.BlockSpec(memory_space=pl.ANY)
    vmem_spec = pl.BlockSpec(memory_space=pltpu.VMEM)
    dma = pltpu.SemaphoreType.DMA
    return pl.pallas_call(
        functools.partial(kernel, n_ctx, n_mp, chunk),
        out_shape=jax.ShapeDtypeStruct((rows, cols), BF16),
        in_specs=[any_spec, any_spec, any_spec, vmem_spec, vmem_spec, any_spec],
        out_specs=any_spec,
        scratch_shapes=[
            pltpu.VMEM((rows, width), BF16), pltpu.VMEM((rows, width), BF16), pltpu.VMEM((rows, width), BF16),
            pltpu.VMEM(out_weight.shape, BF16),
            pltpu.VMEM((rows, HEAD), F32),
            pltpu.VMEM((rows, rows), BF16),
            pltpu.VMEM((n_ctx, width + 8, HEAD), F32),
            pltpu.VMEM((width, 2 * HEAD), BF16),
            pltpu.VMEM((n_mp, rows, width), BF16),
            pltpu.VMEM((rows, cols), BF16),
            dma((4,)), dma((n_chunk,)), dma((n_ctx - 1,)), dma((n_ctx - 1,)),
            dma((n_mp - 1, n_chunk)), dma((n_mp - 1, n_chunk)),
        ],
        compiler_params=pltpu.CompilerParams(collective_id=0, has_side_effects=True, vmem_limit_bytes=56 << 20),
        cost_estimate=pl.CostEstimate(flops=7 * 10**9, bytes_accessed=9 << 20, transcendentals=1 << 20),
    )(queries, keys, values, segment_ids.reshape(1, rows), norm_gain.reshape(1, width), out_weight)


def solution(mesh):
    in_specs = (
        P(("dp", "ctx"), "mp"),
        P(("dp", "ctx"), "mp"),
        P(("dp", "ctx"), "mp"),
        P(("dp", "ctx")),
        P("mp"),
        P(None, "mp"),
    )
    out_specs = P(("dp", "ctx"), "mp")
    return jax.shard_map(
        per_device, mesh=mesh, in_specs=in_specs, out_specs=out_specs, check_vma=False
    )
```

```python
import functools

import jax
import jax.numpy as jnp
from jax import lax
from jax.experimental import pallas as pl
from jax.experimental.pallas import tpu as pltpu
from jax.sharding import PartitionSpec as P

HEAD = 128
MESH = pl.DeviceIdType.MESH
F32, BF16 = jnp.float32, jnp.bfloat16


def features(raw):
    x = raw.astype(F32)
    return jnp.where(x > 0, x + 1.0, jnp.exp(jnp.minimum(x, 0.0))).astype(BF16)


def nn(a, b):
    return lax.dot_general(a, b, (((1,), (0,)), ((), ())), preferred_element_type=F32)


def nt(a, b):
    return lax.dot_general(a, b, (((1,), (1,)), ((), ())), preferred_element_type=F32)


def tn(a, b):
    return lax.dot_general(a, b, (((0,), (0,)), ((), ())), preferred_element_type=F32)


def kernel(n_ctx, n_mp, chunk, piece, q_hbm, k_hbm, v_hbm, seg_ref, gain_ref, w_hbm, out_hbm,
           q, k, v, w, seg_col, mask, state, carry, hid, out_buf,
           load_sem, out_sem, st_send, st_recv, h_send, h_recv):
    ctx, mp = lax.axis_index("ctx"), lax.axis_index("mp")
    rows, width = q.shape
    heads = width // HEAD
    n_chunk = rows // chunk
    loads = []
    for i, (src, dst) in enumerate(((k_hbm, k), (v_hbm, v), (q_hbm, q), (w_hbm, w))):
        c = pltpu.make_async_copy(src, dst, load_sem.at[i])
        c.start()
        loads.append(c)
    barrier = pltpu.get_barrier_semaphore()
    for d in range(1, n_mp):
        pl.semaphore_signal(barrier, inc=1, device_id={"mp": lax.rem(mp + d, n_mp)}, device_id_type=MESH)
    for d in range(1, n_ctx):
        pl.semaphore_signal(barrier, inc=1, device_id={"ctx": lax.rem(ctx + d, n_ctx)}, device_id_type=MESH)

    seg_row = seg_ref[...].astype(F32)
    seg_col[...] = jnp.transpose(jnp.broadcast_to(seg_row, (HEAD, rows)))
    first = seg_col[0:1, :]
    last = seg_col[rows - 1:rows, :]
    in_final = (seg_col[...] == last).astype(BF16)

    loads[0].wait()
    k[...] = features(k[...])
    loads[1].wait()
    for h in range(heads):
        cols = slice(h * HEAD, (h + 1) * HEAD)
        state[ctx, h * HEAD:(h + 1) * HEAD, :] = tn(k[:, cols] * in_final, v[:, cols])
    state[ctx, width:width + 8, :] = jnp.broadcast_to(last, (8, HEAD))
    pl.semaphore_wait(barrier, n_mp - 1 + n_ctx - 1)
    st_copies = []
    for d in range(1, n_ctx):
        c = pltpu.make_async_remote_copy(
            src_ref=state.at[ctx], dst_ref=state.at[ctx], send_sem=st_send.at[d - 1], recv_sem=st_recv.at[d - 1],
            device_id={"ctx": lax.rem(ctx + d, n_ctx)}, device_id_type=MESH)
        c.start()
        st_copies.append(c)

    for i in range(n_chunk):
        r0, r1 = i * chunk, (i + 1) * chunk
        for j in range(r1 // HEAD):
            s0 = j * HEAD
            t = lax.broadcasted_iota(jnp.int32, (chunk, HEAD), 0) + r0
            s = lax.broadcasted_iota(jnp.int32, (chunk, HEAD), 1) + s0
            same = seg_col[r0:r1, :] == seg_row[:, s0:s0 + HEAD]
            mask[r0:r1, s0:s0 + HEAD] = jnp.where(same & (s <= t), 1.0, 0.0).astype(BF16)
    loads[2].wait()
    q[...] = features(q[...])

    for c in st_copies:
        c.wait()
    total = jnp.zeros((width, HEAD), F32)
    for j in range(n_ctx):
        link = (state[j, width:width + 1, :] == first).astype(F32) * (j < ctx).astype(F32)
        total = total + state[j, 0:width, :] * link
    hi = total.astype(BF16)
    carry[:, 0:HEAD] = hi
    carry[:, HEAD:2 * HEAD] = (total - hi.astype(F32)).astype(BF16)

    pair = mp + 1 - 2 * lax.rem(mp, 2)
    across = n_mp - 1 - mp
    beside = across + 1 - 2 * lax.rem(across, 2)
    is_end = (mp == 0) | (mp == n_mp - 1)
    inner = jnp.logical_not(is_end)

    def move(slot, c, way, lane, target):
        part = hid.at[slot, pl.ds(c * piece, piece)]
        return pltpu.make_async_remote_copy(
            src_ref=part, dst_ref=part, send_sem=h_send.at[way, c], recv_sem=h_recv.at[lane, c],
            device_id={"mp": target}, device_id_type=MESH)

    per = chunk // piece
    for i in range(n_chunk):
        r0, r1 = i * chunk, (i + 1) * chunk
        on = (seg_col[r0:r1, :] == first).astype(F32)
        for h in range(heads):
            cols = slice(h * HEAD, (h + 1) * HEAD)
            fq = q[r0:r1, cols]
            score = nt(fq, k[0:r1, cols]).astype(BF16) * mask[r0:r1, 0:r1]
            inside = nn(score, v[0:r1, cols])
            both = nn(fq, carry[cols, :])
            numer = inside + on * (both[:, 0:HEAD] + both[:, HEAD:2 * HEAD])
            mean = jnp.mean(numer * numer, axis=-1, keepdims=True)
            hid[mp, r0:r1, cols] = (numer * lax.rsqrt(mean + 1e-6) * gain_ref[:, cols]).astype(BF16)
        for c in range(i * per, (i + 1) * per):
            move(mp, c, 0, 0, pair).start()

            @pl.when(inner)
            def _():
                move(mp, c, 1, 1, across).start()

    loads[3].wait()

    def project(c):
        r0 = c * piece
        acc = nn(hid[0, pl.ds(r0, piece), :], w[0:width, :])
        for p in range(1, n_mp):
            acc = acc + nn(hid[p, pl.ds(r0, piece), :], w[p * width:(p + 1) * width, :])
        out_buf[pl.ds(r0, piece), :] = acc.astype(BF16)
        pltpu.make_async_copy(out_buf.at[pl.ds(r0, piece)], out_hbm.at[pl.ds(r0, piece)], out_sem.at[c]).start()

    n_piece = rows // piece

    @pl.loop(0, n_piece)
    def _(c):
        move(pair, c, 0, 0, pair).wait_recv()

        @pl.when(inner)
        def _():
            move(pair, c, 2, 2, across).start()
        move(across, c, 0, 1, pair).wait_recv()

        @pl.when(inner)
        def _():
            move(across, c, 3, 1, pair).start()
        move(beside, c, 0, 2, pair).wait_recv()

        @pl.when(inner)
        def _():
            move(beside, c, 4, 2, pair).start()
        project(c)

    @pl.loop(0, n_piece)
    def _(c):
        move(mp, c, 0, 0, pair).wait_send()

        @pl.when(inner)
        def _():
            move(mp, c, 1, 1, across).wait_send()
            move(pair, c, 2, 2, across).wait_send()
            move(across, c, 3, 1, pair).wait_send()
            move(beside, c, 4, 2, pair).wait_send()
        pltpu.make_async_copy(
            out_buf.at[pl.ds(c * piece, piece)], out_hbm.at[pl.ds(c * piece, piece)], out_sem.at[c]).wait()


def per_device(queries, keys, values, segment_ids, norm_gain, out_weight):
    n_ctx, n_mp = lax.axis_size("ctx"), lax.axis_size("mp")
    rows, width = queries.shape
    cols = out_weight.shape[1]
    chunk, piece = 256, 128
    n_piece = rows // piece
    any_spec = pl.BlockSpec(memory_space=pl.ANY)
    vmem_spec = pl.BlockSpec(memory_space=pltpu.VMEM)
    dma = pltpu.SemaphoreType.DMA
    return pl.pallas_call(
        functools.partial(kernel, n_ctx, n_mp, chunk, piece),
        out_shape=jax.ShapeDtypeStruct((rows, cols), BF16),
        in_specs=[any_spec, any_spec, any_spec, vmem_spec, vmem_spec, any_spec],
        out_specs=any_spec,
        scratch_shapes=[
            pltpu.VMEM((rows, width), BF16), pltpu.VMEM((rows, width), BF16), pltpu.VMEM((rows, width), BF16),
            pltpu.VMEM(out_weight.shape, BF16),
            pltpu.VMEM((rows, HEAD), F32),
            pltpu.VMEM((rows, rows), BF16),
            pltpu.VMEM((n_ctx, width + 8, HEAD), F32),
            pltpu.VMEM((width, 2 * HEAD), BF16),
            pltpu.VMEM((n_mp, rows, width), BF16),
            pltpu.VMEM((rows, cols), BF16),
            dma((4,)), dma((n_piece,)), dma((n_ctx - 1,)), dma((n_ctx - 1,)),
            dma((5, n_piece)), dma((3, n_piece)),
        ],
        compiler_params=pltpu.CompilerParams(collective_id=0, has_side_effects=True, vmem_limit_bytes=56 << 20),
        cost_estimate=pl.CostEstimate(flops=7 * 10**9, bytes_accessed=9 << 20, transcendentals=1 << 20),
    )(queries, keys, values, segment_ids.reshape(1, rows), norm_gain.reshape(1, width), out_weight)


def solution(mesh):
    in_specs = (
        P(("dp", "ctx"), "mp"),
        P(("dp", "ctx"), "mp"),
        P(("dp", "ctx"), "mp"),
        P(("dp", "ctx")),
        P("mp"),
        P(None, "mp"),
    )
    out_specs = P(("dp", "ctx"), "mp")
    return jax.shard_map(
        per_device, mesh=mesh, in_specs=in_specs, out_specs=out_specs, check_vma=False
    )
```

```python
import functools

import jax
import jax.numpy as jnp
from jax import lax
from jax.experimental import pallas as pl
from jax.experimental.pallas import tpu as pltpu
from jax.sharding import PartitionSpec as P

HEAD = 128
MESH = pl.DeviceIdType.MESH
F32, BF16 = jnp.float32, jnp.bfloat16


def features(raw):
    x = raw.astype(F32)
    return jnp.where(x > 0, x + 1.0, jnp.exp(jnp.minimum(x, 0.0))).astype(BF16)


def nn(a, b):
    return lax.dot_general(a, b, (((1,), (0,)), ((), ())), preferred_element_type=F32)


def nt(a, b):
    return lax.dot_general(a, b, (((1,), (1,)), ((), ())), preferred_element_type=F32)


def tn(a, b):
    return lax.dot_general(a, b, (((0,), (0,)), ((), ())), preferred_element_type=F32)


def kernel(n_ctx, n_mp, chunk, piece, whole, ahead, q_hbm, k_hbm, v_hbm, seg_ref, gain_ref, w_hbm, out_hbm,
           q, k, v, w, seg_col, mask, state, carry, hid, out_buf,
           wx, part, load_sem, out_sem, st_send, st_recv, h_send, h_recv,
           w_send, w_recv, p_send, p_recv):
    ctx, mp = lax.axis_index("ctx"), lax.axis_index("mp")
    rows, width = q.shape
    heads = width // HEAD
    n_chunk = rows // chunk
    loads = []
    for i, (src, dst) in enumerate(((k_hbm, k), (v_hbm, v), (q_hbm, q), (w_hbm, w))):
        c = pltpu.make_async_copy(src, dst, load_sem.at[i])
        c.start()
        loads.append(c)
    barrier = pltpu.get_barrier_semaphore()
    for d in range(1, n_mp):
        pl.semaphore_signal(barrier, inc=1, device_id={"mp": lax.rem(mp + d, n_mp)}, device_id_type=MESH)
    for d in range(1, n_ctx):
        pl.semaphore_signal(barrier, inc=1, device_id={"ctx": lax.rem(ctx + d, n_ctx)}, device_id_type=MESH)

    dp = lax.axis_index("dp")
    flip = lambda i: i + 1 - 2 * lax.rem(i, 2)
    dp_near, dp_far, twin = flip(dp), lax.rem(dp + 2, 4), flip(ctx)
    for other in (dp_near, dp_far):
        pl.semaphore_signal(barrier, inc=1, device_id={"dp": other}, device_id_type=MESH)
    pair = flip(mp)
    across = n_mp - 1 - mp
    beside = flip(across)
    is_end = (mp == 0) | (mp == n_mp - 1)
    inner = jnp.logical_not(is_end)
    low = lax.rem(ctx, 2)
    mine = dp * 2 + low
    strip = wx.shape[2]

    seg_row = seg_ref[...].astype(F32)
    seg_col[...] = jnp.transpose(jnp.broadcast_to(seg_row, (HEAD, rows)))
    first = seg_col[0:1, :]
    last = seg_col[rows - 1:rows, :]
    in_final = (seg_col[...] == last).astype(BF16)

    loads[0].wait()
    k[...] = features(k[...])
    loads[1].wait()
    for h in range(heads):
        cols = slice(h * HEAD, (h + 1) * HEAD)
        state[ctx, h * HEAD:(h + 1) * HEAD, :] = tn(k[:, cols] * in_final, v[:, cols])
    state[ctx, width:width + 8, :] = jnp.broadcast_to(last, (8, HEAD))
    pl.semaphore_wait(barrier, n_mp - 1 + n_ctx - 1 + 2)

    def lend(n, block):
        return pltpu.make_async_remote_copy(
            src_ref=w_hbm.at[pl.ds(pl.multiple_of(block * width + mine * strip, strip), strip)], dst_ref=wx.at[mine, n],
            send_sem=w_send.at[n], recv_sem=w_recv.at[n], device_id={"mp": pair}, device_id_type=MESH)

    def share(g, n, to):
        return pltpu.make_async_remote_copy(
            src_ref=wx.at[g], dst_ref=wx.at[g], send_sem=w_send.at[n], recv_sem=w_recv.at[n],
            device_id=to, device_id_type=MESH)

    near, far, core = {"dp": dp_near}, {"dp": dp_far}, {"ctx": twin}
    got = (mine, dp_near * 2 + low, dp_far * 2 + low, flip(dp_far) * 2 + low)
    lent = [lend(n, block) for n, block in enumerate((pair, beside, across))]
    shares = [share(got[0], 3, near), share(got[0], 4, far), share(got[1], 5, far)] + [
        share(got[j], 6 + j, core) for j in range(4)]

    @pl.when(is_end)
    def _():
        for c in lent:
            c.start()
    st_copies = []
    for d in range(1, n_ctx):
        c = pltpu.make_async_remote_copy(
            src_ref=state.at[ctx], dst_ref=state.at[ctx], send_sem=st_send.at[d - 1], recv_sem=st_recv.at[d - 1],
            device_id={"ctx": lax.rem(ctx + d, n_ctx)}, device_id_type=MESH)
        c.start()
        st_copies.append(c)

    for i in range(n_chunk):
        r0, r1 = i * chunk, (i + 1) * chunk
        for j in range(r1 // HEAD):
            s0 = j * HEAD
            t = lax.broadcasted_iota(jnp.int32, (chunk, HEAD), 0) + r0
            s = lax.broadcasted_iota(jnp.int32, (chunk, HEAD), 1) + s0
            same = seg_col[r0:r1, :] == seg_row[:, s0:s0 + HEAD]
            mask[r0:r1, s0:s0 + HEAD] = jnp.where(same & (s <= t), 1.0, 0.0).astype(BF16)
    loads[2].wait()
    q[...] = features(q[...])

    for c in st_copies:
        c.wait()
    total = jnp.zeros((width, HEAD), F32)
    for j in range(n_ctx):
        link = (state[j, width:width + 1, :] == first).astype(F32) * (j < ctx).astype(F32)
        total = total + state[j, 0:width, :] * link
    hi = total.astype(BF16)
    carry[:, 0:HEAD] = hi
    carry[:, HEAD:2 * HEAD] = (total - hi.astype(F32)).astype(BF16)

    def move(slot, c, way, lane, target):
        part = hid.at[slot, pl.ds(c * piece, piece)]
        return pltpu.make_async_remote_copy(
            src_ref=part, dst_ref=part, send_sem=h_send.at[way, c], recv_sem=h_recv.at[lane, c],
            device_id={"mp": target}, device_id_type=MESH)

    per = chunk // piece
    for i in range(n_chunk):
        r0, r1 = i * chunk, (i + 1) * chunk
        on = (seg_col[r0:r1, :] == first).astype(F32)
        for h in range(heads):
            cols = slice(h * HEAD, (h + 1) * HEAD)
            fq = q[r0:r1, cols]
            score = nt(fq, k[0:r1, cols]).astype(BF16) * mask[r0:r1, 0:r1]
            inside = nn(score, v[0:r1, cols])
            both = nn(fq, carry[cols, :])
            numer = inside + on * (both[:, 0:HEAD] + both[:, HEAD:2 * HEAD])
            mean = jnp.mean(numer * numer, axis=-1, keepdims=True)
            hid[mp, r0:r1, cols] = (numer * lax.rsqrt(mean + 1e-6) * gain_ref[:, cols]).astype(BF16)
        for c in range(i * per, (i + 1) * per):
            @pl.when(is_end | (c in whole))
            def _():
                move(mp, c, 0, 0, pair).start()

            if c < ahead:
                @pl.when(inner)
                def _():
                    move(mp, c, 1, 1, across).start()

    loads[3].wait()
    n_piece = rows // piece

    def store(c, acc):
        r0 = c * piece
        out_buf[r0:r0 + piece, :] = acc.astype(BF16)
        pltpu.make_async_copy(out_buf.at[pl.ds(r0, piece)], out_hbm.at[pl.ds(r0, piece)], out_sem.at[c]).start()

    def project(c):
        r0 = c * piece
        acc = nn(hid[0, r0:r0 + piece, :], w[0:width, :])
        for p in range(1, n_mp):
            acc = acc + nn(hid[p, r0:r0 + piece, :], w[p * width:(p + 1) * width, :])
        store(c, acc)

    def hand(c):
        return pltpu.make_async_remote_copy(
            src_ref=part.at[c], dst_ref=part.at[c], send_sem=p_send.at[c], recv_sem=p_recv.at[c],
            device_id={"mp": pair}, device_id_type=MESH)

    @pl.when(inner)
    def _():
        for c in lent:
            c.wait_recv()
        for n in (0, 1, 3):
            shares[n].start()
        move(pair, 0, 0, 0, pair).wait_recv()
        move(pair, 0, 2, 2, across).start()
        for c in range(n_piece):
            if c + 1 < n_piece:
                move(pair, c + 1, 0, 0, pair).wait_recv()
                move(pair, c + 1, 2, 2, across).start()
            if c + ahead < n_piece:
                move(mp, c + ahead, 1, 1, across).start()
            if c == 1:
                shares[0].wait_recv()
                shares[2].start()
                shares[4].start()
                shares[1].wait_recv()
                shares[5].start()
            if c == 2:
                shares[2].wait_recv()
                shares[6].start()
            move(across, c, 0, 1, pair).wait_recv()
            if c in whole:
                move(across, c, 3, 1, pair).start()
            move(beside, c, 0, 2, pair).wait_recv()
            if c in whole:
                move(beside, c, 4, 2, pair).start()
            else:
                if c == 2:
                    for n in range(3, 7):
                        shares[n].wait_recv()
                r0 = c * piece
                acc = None
                for n, slot in enumerate((mp, across, beside)):
                    term = nn(hid[slot, r0:r0 + piece, :], wx[:, n].reshape(width, -1))
                    acc = term if acc is None else acc + term
                part[c] = acc.astype(BF16)
                hand(c).start()
            project(c)
        for c in range(n_piece):
            move(mp, c, 1, 1, across).wait_send()
            move(pair, c, 2, 2, across).wait_send()
            if c in whole:
                move(mp, c, 0, 0, pair).wait_send()
                move(across, c, 3, 1, pair).wait_send()
                move(beside, c, 4, 2, pair).wait_send()
            else:
                hand(c).wait_send()
        for c in shares:
            c.wait_send()

    @pl.when(is_end)
    def _():
        for c in range(n_piece):
            if c in whole:
                for lane in range(3):
                    move(across, c, 0, lane, pair).wait_recv()
                project(c)
            else:
                r0 = c * piece
                own = nn(hid[mp, r0:r0 + piece, :], w[pl.ds(pl.multiple_of(mp * width, width), width), :])
                hand(c).wait_recv()
                store(c, own + part[c].astype(F32))
        for c in range(n_piece):
            move(mp, c, 0, 0, pair).wait_send()
        for c in lent:
            c.wait_send()

    for c in range(n_piece):
        pltpu.make_async_copy(
            out_buf.at[pl.ds(c * piece, piece)], out_hbm.at[pl.ds(c * piece, piece)], out_sem.at[c]).wait()


def per_device(queries, keys, values, segment_ids, norm_gain, out_weight):
    n_ctx, n_mp = lax.axis_size("ctx"), lax.axis_size("mp")
    rows, width = queries.shape
    cols = out_weight.shape[1]
    chunk, piece = 256, 128
    n_piece = rows // piece
    whole, ahead = (0, 1, n_piece - 1), 2
    group = 8
    any_spec = pl.BlockSpec(memory_space=pl.ANY)
    vmem_spec = pl.BlockSpec(memory_space=pltpu.VMEM)
    dma = pltpu.SemaphoreType.DMA
    return pl.pallas_call(
        functools.partial(kernel, n_ctx, n_mp, chunk, piece, whole, ahead),
        out_shape=jax.ShapeDtypeStruct((rows, cols), BF16),
        in_specs=[any_spec, any_spec, any_spec, vmem_spec, vmem_spec, any_spec],
        out_specs=any_spec,
        scratch_shapes=[
            pltpu.VMEM((rows, width), BF16), pltpu.VMEM((rows, width), BF16), pltpu.VMEM((rows, width), BF16),
            pltpu.VMEM(out_weight.shape, BF16),
            pltpu.VMEM((rows, HEAD), F32),
            pltpu.VMEM((rows, rows), BF16),
            pltpu.VMEM((n_ctx, width + 8, HEAD), F32),
            pltpu.VMEM((width, 2 * HEAD), BF16),
            pltpu.VMEM((n_mp, rows, width), BF16),
            pltpu.VMEM((rows, cols), BF16),
            pltpu.VMEM((group, n_mp - 1, width // group, cols), BF16),
            pltpu.VMEM((n_piece, piece, cols), BF16),
            dma((4,)), dma((n_piece,)), dma((n_ctx - 1,)), dma((n_ctx - 1,)),
            dma((5, n_piece)), dma((3, n_piece)),
            dma((10,)), dma((10,)), dma((n_piece,)), dma((n_piece,)),
        ],
        compiler_params=pltpu.CompilerParams(collective_id=0, has_side_effects=True, vmem_limit_bytes=56 << 20),
        cost_estimate=pl.CostEstimate(flops=7 * 10**9, bytes_accessed=9 << 20, transcendentals=1 << 20),
    )(queries, keys, values, segment_ids.reshape(1, rows), norm_gain.reshape(1, width), out_weight)


def solution(mesh):
    in_specs = (
        P(("dp", "ctx"), "mp"),
        P(("dp", "ctx"), "mp"),
        P(("dp", "ctx"), "mp"),
        P(("dp", "ctx")),
        P("mp"),
        P(None, "mp"),
    )
    out_specs = P(("dp", "ctx"), "mp")
    return jax.shard_map(
        per_device, mesh=mesh, in_specs=in_specs, out_specs=out_specs, check_vma=False
    )
```

```python
import functools

import jax
import jax.numpy as jnp
from jax import lax
from jax.experimental import pallas as pl
from jax.experimental.pallas import tpu as pltpu
from jax.sharding import PartitionSpec as P

HEAD = 128
MESH = pl.DeviceIdType.MESH
F32, BF16 = jnp.float32, jnp.bfloat16


def features(raw):
    x = raw.astype(F32)
    return jnp.where(x > 0, x + 1.0, jnp.exp(jnp.minimum(x, 0.0))).astype(BF16)


def nn(a, b):
    return lax.dot_general(a, b, (((1,), (0,)), ((), ())), preferred_element_type=F32)


def nt(a, b):
    return lax.dot_general(a, b, (((1,), (1,)), ((), ())), preferred_element_type=F32)


def tn(a, b):
    return lax.dot_general(a, b, (((0,), (0,)), ((), ())), preferred_element_type=F32)


def kernel(n_ctx, n_mp, chunk, piece, whole, ahead, q_hbm, k_hbm, v_hbm, seg_ref, gain_ref, w_hbm, out_hbm,
           q, k, v, w, seg_col, mask, state, carry, hid, out_buf,
           wx, part, load_sem, out_sem, st_send, st_recv, h_send, h_recv,
           w_send, w_recv, p_send, p_recv):
    ctx, mp = lax.axis_index("ctx"), lax.axis_index("mp")
    rows, width = q.shape
    heads = width // HEAD
    n_chunk = rows // chunk
    loads = []
    for i, (src, dst) in enumerate(((k_hbm, k), (v_hbm, v), (q_hbm, q), (w_hbm, w))):
        c = pltpu.make_async_copy(src, dst, load_sem.at[i])
        c.start()
        loads.append(c)
    barrier = pltpu.get_barrier_semaphore()
    for d in range(1, n_mp):
        pl.semaphore_signal(barrier, inc=1, device_id={"mp": lax.rem(mp + d, n_mp)}, device_id_type=MESH)
    for d in range(1, n_ctx):
        pl.semaphore_signal(barrier, inc=1, device_id={"ctx": lax.rem(ctx + d, n_ctx)}, device_id_type=MESH)

    dp = lax.axis_index("dp")
    flip = lambda i: i + 1 - 2 * lax.rem(i, 2)
    dp_near, dp_far, twin = flip(dp), lax.rem(dp + 2, 4), flip(ctx)
    for other in (dp_near, dp_far):
        pl.semaphore_signal(barrier, inc=1, device_id={"dp": other}, device_id_type=MESH)
    pair = flip(mp)
    across = n_mp - 1 - mp
    beside = flip(across)
    is_end = (mp == 0) | (mp == n_mp - 1)
    inner = jnp.logical_not(is_end)
    low = lax.rem(ctx, 2)
    mine = dp * 2 + low
    strip = wx.shape[2]

    seg_row = seg_ref[...].astype(F32)
    seg_col[...] = jnp.transpose(jnp.broadcast_to(seg_row, (HEAD, rows)))
    first = seg_col[0:1, :]
    last = seg_col[rows - 1:rows, :]
    in_final = (seg_col[...] == last).astype(BF16)

    loads[0].wait()
    k[...] = features(k[...])
    loads[1].wait()
    for h in range(heads):
        cols = slice(h * HEAD, (h + 1) * HEAD)
        state[ctx, h * HEAD:(h + 1) * HEAD, :] = tn(k[:, cols] * in_final, v[:, cols])
    state[ctx, width:width + 8, :] = jnp.broadcast_to(last, (8, HEAD))
    pl.semaphore_wait(barrier, n_mp - 1 + n_ctx - 1 + 2)

    def lend(n, block):
        return pltpu.make_async_remote_copy(
            src_ref=w_hbm.at[pl.ds(pl.multiple_of(block * width + mine * strip, strip), strip)], dst_ref=wx.at[mine, n],
            send_sem=w_send.at[n], recv_sem=w_recv.at[n], device_id={"mp": pair}, device_id_type=MESH)

    def share(g, n, to):
        return pltpu.make_async_remote_copy(
            src_ref=wx.at[g], dst_ref=wx.at[g], send_sem=w_send.at[n], recv_sem=w_recv.at[n],
            device_id=to, device_id_type=MESH)

    near, far, core = {"dp": dp_near}, {"dp": dp_far}, {"ctx": twin}
    got = (mine, dp_near * 2 + low, dp_far * 2 + low, flip(dp_far) * 2 + low)
    lent = [lend(n, block) for n, block in enumerate((pair, beside, across))]
    shares = [share(got[0], 3, near), share(got[0], 4, far), share(got[1], 5, far)] + [
        share(got[j], 6 + j, core) for j in range(4)]

    @pl.when(is_end)
    def _():
        for c in lent:
            c.start()
    st_copies = []
    for d in range(1, n_ctx):
        c = pltpu.make_async_remote_copy(
            src_ref=state.at[ctx], dst_ref=state.at[ctx], send_sem=st_send.at[d - 1], recv_sem=st_recv.at[d - 1],
            device_id={"ctx": lax.rem(ctx + d, n_ctx)}, device_id_type=MESH)
        c.start()
        st_copies.append(c)

    for i in range(n_chunk):
        r0, r1 = i * chunk, (i + 1) * chunk
        for j in range(r1 // HEAD):
            s0 = j * HEAD
            t = lax.broadcasted_iota(jnp.int32, (chunk, HEAD), 0) + r0
            s = lax.broadcasted_iota(jnp.int32, (chunk, HEAD), 1) + s0
            same = seg_col[r0:r1, :] == seg_row[:, s0:s0 + HEAD]
            mask[r0:r1, s0:s0 + HEAD] = jnp.where(same & (s <= t), 1.0, 0.0).astype(BF16)
    loads[2].wait()
    q[...] = features(q[...])

    for c in st_copies:
        c.wait()
    total = jnp.zeros((width, HEAD), F32)
    for j in range(n_ctx):
        link = (state[j, width:width + 1, :] == first).astype(F32) * (j < ctx).astype(F32)
        total = total + state[j, 0:width, :] * link
    hi = total.astype(BF16)
    carry[:, 0:HEAD] = hi
    carry[:, HEAD:2 * HEAD] = (total - hi.astype(F32)).astype(BF16)

    def move(slot, c, way, lane, target):
        part = hid.at[slot, pl.ds(c * piece, piece)]
        return pltpu.make_async_remote_copy(
            src_ref=part, dst_ref=part, send_sem=h_send.at[way, c], recv_sem=h_recv.at[lane, c],
            device_id={"mp": target}, device_id_type=MESH)

    per = chunk // piece
    for i in range(n_chunk):
        r0, r1 = i * chunk, (i + 1) * chunk
        on = (seg_col[r0:r1, :] == first).astype(F32)
        for h in range(heads):
            cols = slice(h * HEAD, (h + 1) * HEAD)
            fq = q[r0:r1, cols]
            score = nt(fq, k[0:r1, cols]).astype(BF16) * mask[r0:r1, 0:r1]
            inside = nn(score, v[0:r1, cols])
            both = nn(fq, carry[cols, :])
            numer = inside + on * (both[:, 0:HEAD] + both[:, HEAD:2 * HEAD])
            mean = jnp.mean(numer * numer, axis=-1, keepdims=True)
            hid[mp, r0:r1, cols] = (numer * lax.rsqrt(mean + 1e-6) * gain_ref[:, cols]).astype(BF16)
        for c in range(i * per, (i + 1) * per):
            @pl.when(is_end | (c in whole))
            def _():
                move(mp, c, 0, 0, pair).start()

            if c < ahead:
                @pl.when(inner)
                def _():
                    move(mp, c, 1, 1, across).start()

    loads[3].wait()
    n_piece = rows // piece

    def store(c, acc):
        r0 = c * piece
        out_buf[r0:r0 + piece, :] = acc.astype(BF16)
        pltpu.make_async_copy(out_buf.at[pl.ds(r0, piece)], out_hbm.at[pl.ds(r0, piece)], out_sem.at[c]).start()

    def project(c):
        r0 = c * piece
        acc = nn(hid[0, r0:r0 + piece, :], w[0:width, :])
        for p in range(1, n_mp):
            acc = acc + nn(hid[p, r0:r0 + piece, :], w[p * width:(p + 1) * width, :])
        store(c, acc)

    def hand(c):
        return pltpu.make_async_remote_copy(
            src_ref=part.at[c], dst_ref=part.at[c], send_sem=p_send.at[c], recv_sem=p_recv.at[c],
            device_id={"mp": pair}, device_id_type=MESH)

    @pl.when(inner)
    def _():
        for c in lent:
            c.wait_recv()
        for n in (0, 1, 3):
            shares[n].start()
        move(pair, 0, 0, 0, pair).wait_recv()
        move(pair, 0, 2, 2, across).start()
        for c in range(n_piece):
            if c + 1 < n_piece:
                move(pair, c + 1, 0, 0, pair).wait_recv()
                move(pair, c + 1, 2, 2, across).start()
            if c + ahead < n_piece:
                move(mp, c + ahead, 1, 1, across).start()
            if c == 1:
                shares[0].wait_recv()
                shares[2].start()
                shares[4].start()
                shares[1].wait_recv()
                shares[5].start()
            if c == 2:
                shares[2].wait_recv()
                shares[6].start()
            move(across, c, 0, 1, pair).wait_recv()
            if c in whole:
                move(across, c, 3, 1, pair).start()
            move(beside, c, 0, 2, pair).wait_recv()
            if c in whole:
                move(beside, c, 4, 2, pair).start()
            else:
                if c == whole.index(n_piece - 1):
                    for n in range(3, 7):
                        shares[n].wait_recv()
                r0 = c * piece
                acc = None
                for n, slot in enumerate((mp, across, beside)):
                    term = nn(hid[slot, r0:r0 + piece, :], wx[:, n].reshape(width, -1))
                    acc = term if acc is None else acc + term
                part[c] = acc.astype(BF16)
                hand(c).start()
            project(c)
        for c in range(n_piece):
            move(mp, c, 1, 1, across).wait_send()
            move(pair, c, 2, 2, across).wait_send()
            if c in whole:
                move(mp, c, 0, 0, pair).wait_send()
                move(across, c, 3, 1, pair).wait_send()
                move(beside, c, 4, 2, pair).wait_send()
            else:
                hand(c).wait_send()
        for c in shares:
            c.wait_send()

    @pl.when(is_end)
    def _():
        for c in range(n_piece):
            if c in whole:
                for lane in range(3):
                    move(across, c, 0, lane, pair).wait_recv()
                project(c)
            else:
                r0 = c * piece
                own = nn(hid[mp, r0:r0 + piece, :], w[pl.ds(pl.multiple_of(mp * width, width), width), :])
                hand(c).wait_recv()
                store(c, own + part[c].astype(F32))
        for c in range(n_piece):
            move(mp, c, 0, 0, pair).wait_send()
        for c in lent:
            c.wait_send()

    for c in range(n_piece):
        pltpu.make_async_copy(
            out_buf.at[pl.ds(c * piece, piece)], out_hbm.at[pl.ds(c * piece, piece)], out_sem.at[c]).wait()


def per_device(queries, keys, values, segment_ids, norm_gain, out_weight):
    n_ctx, n_mp = lax.axis_size("ctx"), lax.axis_size("mp")
    rows, width = queries.shape
    cols = out_weight.shape[1]
    chunk, piece = 256, 128
    n_piece = rows // piece
    whole, ahead = (0, 1, 2, n_piece - 1), 4
    group = 8
    any_spec = pl.BlockSpec(memory_space=pl.ANY)
    vmem_spec = pl.BlockSpec(memory_space=pltpu.VMEM)
    dma = pltpu.SemaphoreType.DMA
    return pl.pallas_call(
        functools.partial(kernel, n_ctx, n_mp, chunk, piece, whole, ahead),
        out_shape=jax.ShapeDtypeStruct((rows, cols), BF16),
        in_specs=[any_spec, any_spec, any_spec, vmem_spec, vmem_spec, any_spec],
        out_specs=any_spec,
        scratch_shapes=[
            pltpu.VMEM((rows, width), BF16), pltpu.VMEM((rows, width), BF16), pltpu.VMEM((rows, width), BF16),
            pltpu.VMEM(out_weight.shape, BF16),
            pltpu.VMEM((rows, HEAD), F32),
            pltpu.VMEM((rows, rows), BF16),
            pltpu.VMEM((n_ctx, width + 8, HEAD), F32),
            pltpu.VMEM((width, 2 * HEAD), BF16),
            pltpu.VMEM((n_mp, rows, width), BF16),
            pltpu.VMEM((rows, cols), BF16),
            pltpu.VMEM((group, n_mp - 1, width // group, cols), BF16),
            pltpu.VMEM((n_piece, piece, cols), BF16),
            dma((4,)), dma((n_piece,)), dma((n_ctx - 1,)), dma((n_ctx - 1,)),
            dma((5, n_piece)), dma((3, n_piece)),
            dma((10,)), dma((10,)), dma((n_piece,)), dma((n_piece,)),
        ],
        compiler_params=pltpu.CompilerParams(collective_id=0, has_side_effects=True, vmem_limit_bytes=56 << 20),
        cost_estimate=pl.CostEstimate(flops=7 * 10**9, bytes_accessed=9 << 20, transcendentals=1 << 20),
    )(queries, keys, values, segment_ids.reshape(1, rows), norm_gain.reshape(1, width), out_weight)


def solution(mesh):
    in_specs = (
        P(("dp", "ctx"), "mp"),
        P(("dp", "ctx"), "mp"),
        P(("dp", "ctx"), "mp"),
        P(("dp", "ctx")),
        P("mp"),
        P(None, "mp"),
    )
    out_specs = P(("dp", "ctx"), "mp")
    return jax.shard_map(
        per_device, mesh=mesh, in_specs=in_specs, out_specs=out_specs, check_vma=False
    )
```
